512 devices in a mesh: band: 4 (over x_lo, core), shot: 16 (over x_hi, y), recv: 8 (over z).
Axes of the slice: x: 4 (x_hi: 2, x_lo: 2; x = x_hi * 2 + x_lo), y: 8, z: 8, core: 2. Of those that a mesh axis runs over, the one named last changes fastest.
Arguments:
- traces: float32 [1536, 384, 512], P(('band', 'shot'), 'recv'), parts along dimension 0, may hold values from -6 to 6
Outputs:
- predicted: float32 [1536, 384, 512], P(('band', 'shot'), 'recv'), parts along dimension 0
The draws below stay inside these ranges and needn't reach their ends.
There are 4 independent parts, one for each index of `band`. The reference program is written for one: setup_inputs(seed, part) draws one part's arguments, and reference() takes and returns one part's arrays. A program takes and returns all parts, laid end to end along the dimension named above; each array names one. Nothing has to cross between parts.
All inputs are finite; a program needn't handle non-finite values.
Results may differ from the reference program's by a relative error of at most 0.000094.
Values sent between devices are 32-bit elements; how exact they have to be, the bound alone decides.
A program may use at most 64 MiB of HBM per device.

```python
import math
import jax
import jax.numpy as jnp
from jax import lax

NT = 512
K0 = 32
S = 384
R = 384
NF = 64


def steps_of(own_key, extent, pieces, least, high):
    loudness = 1.0
    for position, blocks in pieces:
        heights = jax.random.uniform(jax.random.fold_in(jax.random.fold_in(own_key, 6), position), (blocks,), jnp.float32, least / len(pieces), high / len(pieces))
        loudness = loudness * jnp.repeat(jnp.exp(heights), extent[position] // blocks).reshape((-1,) + (1,) * (len(extent) - 1 - position))
    return loudness


def noise(key, shape, scale, bound, split=(), kind=jnp.bfloat16):
    level = steps_of(key, shape, split, -0.22, 0.18) if split else 1.0
    entries = jax.random.normal(key, shape, jnp.float32) * scale * level
    return jnp.minimum(jnp.maximum(entries, -bound), bound).astype(kind)


def setup_inputs(seed: int = 0, part: int = 0) -> dict:
    arg_keys = jax.random.split(jax.random.key(seed), 2)
    own_keys = jax.random.split(jax.random.fold_in(arg_keys[1], part), 2)
    return {
        "traces": noise(own_keys[0], (S, R, NT), 1.0, 6.0, ((0, 16), (1, 8)), jnp.float32),
    }


def dft_tables():
    times = jnp.arange(NT, dtype=jnp.int32)
    bins = jnp.arange(NF, dtype=jnp.int32) + K0
    phases = times[:, None] * bins[None, :] % NT
    angles = phases.astype(jnp.float32) * (2.0 * math.pi / NT)
    return (jnp.cos(angles), jnp.sin(angles))

def complex_product(a_real, a_imag, b_real, b_imag):
    hp = lax.Precision.HIGHEST
    real_part = jnp.dot(a_real, b_real, precision=hp) - jnp.dot(a_imag, b_imag, precision=hp)
    imag_part = jnp.dot(a_real, b_imag, precision=hp) + jnp.dot(a_imag, b_real, precision=hp)
    return (real_part, imag_part)

def reference(traces):
    hp = lax.Precision.HIGHEST
    symmetric = 0.5 * (traces + jnp.transpose(traces, (1, 0, 2)))
    cosines, sines = dft_tables()
    forward = jnp.concatenate([cosines, -sines], axis=1) * (1.0 / math.sqrt(NT * S))
    spectrum = jnp.dot(symmetric.reshape(S * R, NT), forward, precision=hp).reshape(S, R, 2, NF)
    spectrum = jnp.transpose(spectrum, (3, 2, 0, 1))

    def per_bin(matrix):
        square_re, square_im = complex_product(matrix[0], matrix[1], matrix[0], matrix[1])
        cube_re, cube_im = complex_product(matrix[0], matrix[1], square_re, square_im)
        return jnp.stack([matrix[0] + square_re + cube_re, matrix[1] + square_im + cube_im])
    totals = lax.map(per_bin, spectrum)
    flat = jnp.transpose(totals, (2, 3, 1, 0)).reshape(S * R, 2 * NF)
    inverse = jnp.concatenate([cosines.T, -sines.T], axis=0) * (2.0 * math.sqrt(S / NT))
    return jnp.dot(flat, inverse, precision=hp).reshape(S, R, NT)
```

```python
import functools
import math

import jax
import jax.numpy as jnp
import numpy as np
from jax import lax
from jax.experimental import pallas as pl
from jax.experimental.pallas import tpu as pltpu
from jax.sharding import PartitionSpec as P

K0 = 32
NT = 512
NF = 64
SIZE = 384
SHOTS = 16
RECVS = 8
GROUP = SHOTS * RECVS
ROWS = SIZE // SHOTS
COLS = SIZE // RECVS
LANES = 128
PIECES = 9
F32 = jnp.float32
BF16 = jnp.bfloat16
MESH = pl.DeviceIdType.MESH


def split_np(table):
    high = table.astype(BF16)
    low = (table - high.astype(np.float32)).astype(BF16)
    return high, low


def tables():
    times = np.arange(NT)
    bins = np.arange(NF) + K0
    angles = (times[:, None] * bins[None, :] % NT) * (2.0 * math.pi / NT)
    cosines, sines = np.cos(angles), np.sin(angles)
    forward = np.concatenate([cosines, -sines], axis=1) / math.sqrt(NT * SIZE)
    inverse = np.concatenate([cosines.T, -sines.T], axis=0) * (2.0 * math.sqrt(SIZE / NT))
    f_high, f_low = split_np(forward.astype(np.float32))
    i_high, i_low = split_np(inverse.astype(np.float32))
    return np.concatenate([f_high, f_low], axis=1), np.concatenate([i_high, i_high, i_low], axis=0)


def split(value):
    high = value.astype(BF16)
    low = (value - high.astype(F32)).astype(BF16)
    return high, low


def dot(a, b):
    return jnp.dot(a, b, preferred_element_type=F32)


def exchange(regs):
    lane = lax.broadcasted_iota(jnp.int32, (8, LANES), 1)
    for bit in (1, 2, 4):
        upper = (lane & bit) != 0
        fresh = list(regs)
        for v in range(8):
            if v & bit:
                continue
            low, high = regs[v], regs[v | bit]
            fresh[v] = jnp.where(upper, pltpu.roll(high, bit, 1), low)
            fresh[v | bit] = jnp.where(upper, high, pltpu.roll(low, LANES - bit, 1))
        regs = fresh
    return regs


def owner_kernel(
    traces, table, back,
    tile, spec, stage, land, raw, sym, d_high, d_low, n_high, n_low, total, leave,
    load_sem, send_sem, recv_sem, own_sem, send2_sem, recv2_sem, own2_sem,
):
    band, shot, recv = lax.axis_index("band"), lax.axis_index("shot"), lax.axis_index("recv")
    parity = lax.rem(band, 2)
    me = shot * RECVS + recv
    is_owner = lax.rem(shot + recv + parity, 2) == 0
    my_bin = shot * 4 + recv // 2
    my_slot = (lax.rem(shot, 2) * 8 + recv) * 8 + shot // 2

    loads = []
    for third in range(3):
        part = pl.ds(third * 8, 8)
        loads.append(pltpu.make_async_copy(traces.at[part], tile.at[part], load_sem.at[third]))
        loads[-1].start()

    barrier = pltpu.get_barrier_semaphore()

    def greet(k, carry):
        other = lax.rem(me + k, GROUP)
        pl.semaphore_signal(
            barrier, inc=1, device_id=(band, other // RECVS, lax.rem(other, RECVS)), device_id_type=MESH
        )
        return carry

    lax.fori_loop(1, GROUP, greet, 0)

    for third in range(3):
        loads[third].wait()
        x_high, x_low = split(tile[pl.ds(third * 8, 8)].reshape(8 * COLS, NT))
        wide = dot(x_high, table[...])
        spec[...] = wide[:, :LANES] + wide[:, LANES:] + dot(x_low, table[:, :LANES])
        for c in range(3):
            rows = [spec[pl.ds(16 * c + m, 8, stride=COLS), :] for m in range(16)]
            turned = jnp.concatenate(rows, axis=0).T
            stage[third * 3 + c] = turned[:NF]
            stage[PIECES + third * 3 + c] = turned[NF:]

    pl.semaphore_wait(barrier, GROUP - 1)

    def send(k, carry):
        step = lax.rem(k * 29, NF)
        to_shot = lax.rem(shot + step // 4, SHOTS)
        to_quad = lax.rem(recv // 2 + step, 4)
        to_recv = 2 * to_quad + lax.rem(to_shot + parity, 2)
        source = stage.at[:, to_shot * 4 + to_quad, :]
        target = land.at[:, my_slot, :]
        mine = (to_shot == shot) & (to_recv == recv)

        @pl.when(mine)
        def _():
            pltpu.make_async_copy(source, target, own_sem).start()

        @pl.when(jnp.logical_not(mine))
        def _():
            pltpu.make_async_remote_copy(
                src_ref=source, dst_ref=target, send_sem=send_sem, recv_sem=recv_sem,
                device_id=(band, to_shot, to_recv), device_id_type=MESH,
            ).start()

        return carry

    lax.fori_loop(0, NF, send, 0)

    @pl.when(is_owner)
    def _():
        one = land.at[:, 0, :]
        pltpu.make_async_copy(one, one, own_sem).wait()
        rest = land.at[:, pl.ds(0, GROUP - 1), :]
        pltpu.make_async_copy(rest, rest, recv_sem).wait()

        for comp in range(2):
            def arrange(block, carry):
                half, third = block // 3, lax.rem(block, 3)
                for c in range(3):
                    regs = [
                        land[comp * PIECES + third * 3 + c, pl.ds(pl.multiple_of((half * 8 + v) * 8, 8), 8), :]
                        for v in range(8)
                    ]
                    regs = exchange(regs)
                    for v in range(8):
                        row = pl.multiple_of((half * 24 + third * 8 + v) * 8, 8)
                        raw[comp, pl.ds(row, 8), c * LANES:(c + 1) * LANES] = regs[v]
                return carry

            lax.fori_loop(0, 6, arrange, 0)

        for comp in range(2):
            for p in range(3):
                for q in range(3):
                    rows, cols = slice(p * LANES, (p + 1) * LANES), slice(q * LANES, (q + 1) * LANES)
                    value = 0.5 * (raw[comp, rows, cols] + raw[comp, cols, rows].T)
                    high, low = split(value)
                    here = slice(comp * SIZE + q * LANES, comp * SIZE + (q + 1) * LANES)
                    there = slice((1 - comp) * SIZE + q * LANES, (1 - comp) * SIZE + (q + 1) * LANES)
                    sym[rows, here] = value
                    d_high[rows, here] = high
                    d_low[rows, here] = low
                    n_high[rows, there] = high if comp == 0 else -high
                    n_low[rows, there] = low if comp == 0 else -low

        def product(high, low):
            out = dot(high[:, :SIZE], d_high[...]) + dot(high[:, SIZE:], n_high[...])
            out += dot(low[:, :SIZE], d_high[...]) + dot(low[:, SIZE:], n_high[...])
            return out + dot(high[:, :SIZE], d_low[...]) + dot(high[:, SIZE:], n_low[...])

        def half_of(half, carry):
            mine = pl.ds(pl.multiple_of(half * 192, 64), 192)
            square = product(d_high[mine, :], d_low[mine, :])
            s_high, s_low = split(square)
            total[...] = sym[mine, :] + square + product(s_high, s_low)

            def scatter(third, carry):
                for comp in range(2):
                    for c in range(3):
                        lanes = slice(comp * SIZE + c * LANES, comp * SIZE + (c + 1) * LANES)
                        regs = [total[pl.ds(pl.multiple_of((third * 8 + v) * 8, 8), 8), lanes] for v in range(8)]
                        regs = exchange(regs)
                        for v in range(8):
                            slot = pl.ds(pl.multiple_of((half * 8 + v) * 8, 8), 8)
                            leave[comp * PIECES + third * 3 + c, slot, :] = regs[v]
                return carry

            lax.fori_loop(0, 3, scatter, 0)

            def reply(k, carry):
                step = lax.rem(k * 29, 64)
                to_shot = lax.rem(shot // 2 + step // 8, 8) * 2 + half
                to_recv = lax.rem(recv + step, 8)
                slot = (half * 8 + to_recv) * 8 + to_shot // 2
                source = leave.at[:, slot, :]
                target = back.at[:, my_bin, :]
                mine = (to_shot == shot) & (to_recv == recv)

                @pl.when(mine)
                def _():
                    pltpu.make_async_copy(source, target, own2_sem).start()

                @pl.when(jnp.logical_not(mine))
                def _():
                    pltpu.make_async_remote_copy(
                        src_ref=source, dst_ref=target, send_sem=send2_sem, recv_sem=recv2_sem,
                        device_id=(band, to_shot, to_recv), device_id_type=MESH,
                    ).start()

                return carry

            lax.fori_loop(0, 64, reply, 0)
            return carry

        lax.fori_loop(0, 2, half_of, 0)

        pltpu.make_async_copy(stage.at[:, pl.ds(0, NF - 1), :], stage.at[:, pl.ds(0, NF - 1), :], send_sem).wait()
        one = back.at[:, 0, :]
        pltpu.make_async_copy(one, one, own2_sem).wait()
        rest = back.at[:, pl.ds(0, NF - 1), :]
        pltpu.make_async_copy(rest, rest, recv2_sem).wait()
        rest = leave.at[:, pl.ds(0, GROUP - 1), :]
        pltpu.make_async_copy(rest, rest, send2_sem).wait()

    @pl.when(jnp.logical_not(is_owner))
    def _():
        pltpu.make_async_copy(stage, stage, send_sem).wait()
        pltpu.make_async_copy(back, back, recv2_sem).wait()


def inverse_kernel(back, table, out, turned):
    third = pl.program_id(0)
    for c in range(3):
        both = jnp.concatenate([back[third * 3 + c], back[PIECES + third * 3 + c]], axis=0)
        turned[...] = both.T
        rows = [turned[pl.ds(a, 16, stride=8), :] for a in range(8)]
        high, low = split(jnp.concatenate(rows, axis=0))
        both = jnp.concatenate([high, low], axis=1)
        value = dot(both, table[:2 * LANES, :]) + dot(high, table[2 * LANES:, :])
        out[:, 16 * c:16 * (c + 1), :] = value.reshape(8, 16, NT)


def body(forward, inverse, traces):
    vmem = pl.BlockSpec(memory_space=pltpu.VMEM)
    back = pl.pallas_call(
        owner_kernel,
        out_shape=jax.ShapeDtypeStruct((2 * PIECES, NF, LANES), F32),
        in_specs=[pl.BlockSpec(memory_space=pl.ANY), vmem],
        out_specs=vmem,
        scratch_shapes=[
            pltpu.VMEM((ROWS, COLS, NT), F32),
            pltpu.VMEM((8 * COLS, LANES), F32),
            pltpu.VMEM((2 * PIECES, NF, LANES), F32),
            pltpu.VMEM((2 * PIECES, GROUP, LANES), F32),
            pltpu.VMEM((2, SIZE, SIZE), F32),
            pltpu.VMEM((SIZE, 2 * SIZE), F32),
            pltpu.VMEM((SIZE, 2 * SIZE), BF16),
            pltpu.VMEM((SIZE, 2 * SIZE), BF16),
            pltpu.VMEM((SIZE, 2 * SIZE), BF16),
            pltpu.VMEM((SIZE, 2 * SIZE), BF16),
            pltpu.VMEM((SIZE // 2, 2 * SIZE), F32),
            pltpu.VMEM((2 * PIECES, GROUP, LANES), F32),
            pltpu.SemaphoreType.DMA((3,)),
        ] + [pltpu.SemaphoreType.DMA] * 6,
        compiler_params=pltpu.CompilerParams(
            collective_id=0, has_side_effects=True, vmem_limit_bytes=40 * 2**20
        ),
    )(traces, forward)
    return pl.pallas_call(
        inverse_kernel,
        grid=(3,),
        out_shape=jax.ShapeDtypeStruct((ROWS, COLS, NT), F32),
        in_specs=[vmem, vmem],
        out_specs=pl.BlockSpec((8, COLS, NT), lambda third: (third, 0, 0)),
        scratch_shapes=[pltpu.VMEM((LANES, LANES), F32)],
        compiler_params=pltpu.CompilerParams(vmem_limit_bytes=20 * 2**20),
    )(back, inverse)


def solution(mesh):
    forward, inverse = tables()
    spec = P(("band", "shot"), "recv", None)
    return jax.shard_map(
        functools.partial(body, jnp.asarray(forward), jnp.asarray(inverse)),
        mesh=mesh, in_specs=(spec,), out_specs=spec, check_vma=False,
    )
```

```python
import functools
import math

import jax
import jax.numpy as jnp
import numpy as np
from jax import lax
from jax.experimental import pallas as pl
from jax.experimental.pallas import tpu as pltpu
from jax.sharding import PartitionSpec as P

K0 = 32
NT = 512
NF = 64
SIZE = 384
SHOTS = 16
RECVS = 8
GROUP = SHOTS * RECVS
ROWS = SIZE // SHOTS
COLS = SIZE // RECVS
LANES = 128
PIECES = 9
F32 = jnp.float32
BF16 = jnp.bfloat16
MESH = pl.DeviceIdType.MESH


def split_np(table):
    high = table.astype(BF16)
    low = (table - high.astype(np.float32)).astype(BF16)
    return high, low


def tables():
    times = np.arange(NT)
    bins = np.arange(NF) + K0
    angles = (times[:, None] * bins[None, :] % NT) * (2.0 * math.pi / NT)
    cosines, sines = np.cos(angles), np.sin(angles)
    forward = np.concatenate([cosines, -sines], axis=1) / math.sqrt(NT * SIZE)
    inverse = np.concatenate([cosines.T, -sines.T], axis=0) * (2.0 * math.sqrt(SIZE / NT))
    f_high, f_low = split_np(forward.astype(np.float32))
    i_high, i_low = split_np(inverse.astype(np.float32))
    return np.concatenate([f_high, f_low], axis=1), np.concatenate([i_high, i_high, i_low], axis=0)


def split(value):
    high = value.astype(BF16)
    low = (value - high.astype(F32)).astype(BF16)
    return high, low


def dot(a, b):
    return jnp.dot(a, b, preferred_element_type=F32)


def exchange(regs):
    lane = lax.broadcasted_iota(jnp.int32, (8, LANES), 1)
    for bit in (1, 2, 4):
        upper = (lane & bit) != 0
        fresh = list(regs)
        for v in range(8):
            if v & bit:
                continue
            low, high = regs[v], regs[v | bit]
            fresh[v] = jnp.where(upper, pltpu.roll(high, bit, 1), low)
            fresh[v | bit] = jnp.where(upper, high, pltpu.roll(low, LANES - bit, 1))
        regs = fresh
    return regs


def owner_kernel(
    traces, table_hbm, back,
    tile, table, spec, stage, land, raw, sym, w_high, w_low, total, leave,
    load_sem, send_sem, recv_sem, own_sem, send2_sem, recv2_sem, own2_sem,
):
    band, shot, recv = lax.axis_index("band"), lax.axis_index("shot"), lax.axis_index("recv")
    parity = lax.rem(band, 2)
    me = shot * RECVS + recv
    is_owner = lax.rem(shot + recv + parity, 2) == 0
    my_bin = shot * 4 + recv // 2
    my_slot = (lax.rem(shot, 2) * 8 + recv) * 8 + shot // 2

    loads = [pltpu.make_async_copy(table_hbm, table, load_sem.at[3])]
    loads[0].start()
    for third in range(3):
        part = pl.ds(third * 8, 8)
        loads.append(pltpu.make_async_copy(traces.at[part], tile.at[part], load_sem.at[third]))
        loads[-1].start()

    barrier = pltpu.get_barrier_semaphore()

    def greet(k, carry):
        other = lax.rem(me + k, GROUP)
        pl.semaphore_signal(
            barrier, inc=1, device_id=(band, other // RECVS, lax.rem(other, RECVS)), device_id_type=MESH
        )
        return carry

    lax.fori_loop(1, GROUP, greet, 0)

    loads[0].wait()
    for third in range(3):
        loads[third + 1].wait()
        x_high, x_low = split(tile[pl.ds(third * 8, 8)].reshape(8 * COLS, NT))
        wide = dot(x_high, table[...])
        spec[...] = wide[:, :LANES] + wide[:, LANES:] + dot(x_low, table[:, :LANES])
        for c in range(3):
            rows = [spec[pl.ds(16 * c + m, 8, stride=COLS), :] for m in range(16)]
            turned = jnp.concatenate(rows, axis=0).T
            stage[third * 3 + c] = turned[:NF]
            stage[PIECES + third * 3 + c] = turned[NF:]

    pl.semaphore_wait(barrier, GROUP - 1)

    def send(k, carry):
        step = lax.rem(k * 29, NF)
        to_shot = lax.rem(shot + step // 4, SHOTS)
        to_quad = lax.rem(recv // 2 + step, 4)
        to_recv = 2 * to_quad + lax.rem(to_shot + parity, 2)
        source = stage.at[:, to_shot * 4 + to_quad, :]
        target = land.at[:, my_slot, :]
        mine = (to_shot == shot) & (to_recv == recv)

        @pl.when(mine)
        def _():
            pltpu.make_async_copy(source, target, own_sem).start()

        @pl.when(jnp.logical_not(mine))
        def _():
            pltpu.make_async_remote_copy(
                src_ref=source, dst_ref=target, send_sem=send_sem, recv_sem=recv_sem,
                device_id=(band, to_shot, to_recv), device_id_type=MESH,
            ).start()

        return carry

    lax.fori_loop(0, NF, send, 0)

    @pl.when(is_owner)
    def _():
        one = land.at[:, 0, :]
        pltpu.make_async_copy(one, one, own_sem).wait()
        rest = land.at[:, pl.ds(0, GROUP - 1), :]
        pltpu.make_async_copy(rest, rest, recv_sem).wait()

        def arrange(block, carry):
            half, third = block // 3, lax.rem(block, 3)
            for comp in range(2):
                for c in range(3):
                    piece = comp * PIECES + third * 3 + c
                    regs = [land[piece, pl.ds(pl.multiple_of((half * 8 + v) * 8, 8), 8), :] for v in range(8)]
                    regs = exchange(regs)
                    for v in range(8):
                        row = pl.multiple_of((half * 24 + third * 8 + v) * 8, 8)
                        raw[comp, pl.ds(row, 8), c * LANES:(c + 1) * LANES] = regs[v]
            return carry

        lax.fori_loop(0, 6, arrange, 0)

        for comp in range(2):
            for p in range(3):
                for q in range(3):
                    rows, cols = slice(p * LANES, (p + 1) * LANES), slice(q * LANES, (q + 1) * LANES)
                    value = 0.5 * (raw[comp, rows, cols] + raw[comp, cols, rows].T)
                    high, low = split(value)
                    below = slice(SIZE + p * LANES, SIZE + (p + 1) * LANES)
                    here = slice(comp * SIZE + q * LANES, comp * SIZE + (q + 1) * LANES)
                    there = slice((1 - comp) * SIZE + q * LANES, (1 - comp) * SIZE + (q + 1) * LANES)
                    sym[rows, here] = value
                    w_high[rows, here] = high
                    w_low[rows, here] = low
                    w_high[below, there] = high if comp == 0 else -high
                    w_low[below, there] = low if comp == 0 else -low

        def product(high, low):
            both = dot(jnp.concatenate([high, low], axis=0), w_high[...])
            return both[:SIZE // 2] + both[SIZE // 2:] + dot(high, w_low[...])

        def half_of(turn, carry):
            half = lax.rem(turn + recv, 2)
            mine = pl.ds(pl.multiple_of(half * 192, 64), 192)
            square = product(w_high[mine, :], w_low[mine, :])
            s_high, s_low = split(square)
            total[...] = sym[mine, :] + square + product(s_high, s_low)
            def scatter(third, carry):
                for comp in range(2):
                    for c in range(3):
                        lanes = slice(comp * SIZE + c * LANES, comp * SIZE + (c + 1) * LANES)
                        regs = [total[pl.ds(pl.multiple_of((third * 8 + v) * 8, 8), 8), lanes] for v in range(8)]
                        regs = exchange(regs)
                        for v in range(8):
                            slot = pl.ds(pl.multiple_of((half * 8 + v) * 8, 8), 8)
                            leave[comp * PIECES + third * 3 + c, slot, :] = regs[v]
                return carry

            lax.fori_loop(0, 3, scatter, 0)

            def reply(k, carry):
                step = lax.rem(k * 29, 64)
                to_shot = lax.rem(shot // 2 + step // 8, 8) * 2 + half
                to_recv = lax.rem(recv + step, 8)
                slot = (half * 8 + to_recv) * 8 + to_shot // 2
                source = leave.at[:, slot, :]
                target = back.at[:, my_bin, :]
                mine = (to_shot == shot) & (to_recv == recv)

                @pl.when(mine)
                def _():
                    pltpu.make_async_copy(source, target, own2_sem).start()

                @pl.when(jnp.logical_not(mine))
                def _():
                    pltpu.make_async_remote_copy(
                        src_ref=source, dst_ref=target, send_sem=send2_sem, recv_sem=recv2_sem,
                        device_id=(band, to_shot, to_recv), device_id_type=MESH,
                    ).start()

                return carry

            lax.fori_loop(0, 64, reply, 0)
            return carry

        lax.fori_loop(0, 2, half_of, 0)

        pltpu.make_async_copy(stage.at[:, pl.ds(0, NF - 1), :], stage.at[:, pl.ds(0, NF - 1), :], send_sem).wait()
        one = back.at[:, 0, :]
        pltpu.make_async_copy(one, one, own2_sem).wait()
        rest = back.at[:, pl.ds(0, NF - 1), :]
        pltpu.make_async_copy(rest, rest, recv2_sem).wait()
        rest = leave.at[:, pl.ds(0, GROUP - 1), :]
        pltpu.make_async_copy(rest, rest, send2_sem).wait()

    @pl.when(jnp.logical_not(is_owner))
    def _():
        pltpu.make_async_copy(stage, stage, send_sem).wait()
        pltpu.make_async_copy(back, back, recv2_sem).wait()


def inverse_kernel(back, table, out, turned):
    third = pl.program_id(0)
    for c in range(3):
        both = jnp.concatenate([back[third * 3 + c], back[PIECES + third * 3 + c]], axis=0)
        turned[...] = both.T
        rows = [turned[pl.ds(a, 16, stride=8), :] for a in range(8)]
        high, low = split(jnp.concatenate(rows, axis=0))
        both = jnp.concatenate([high, low], axis=1)
        value = dot(both, table[:2 * LANES, :]) + dot(high, table[2 * LANES:, :])
        out[:, 16 * c:16 * (c + 1), :] = value.reshape(8, 16, NT)


def body(forward, inverse, traces):
    vmem = pl.BlockSpec(memory_space=pltpu.VMEM)
    back = pl.pallas_call(
        owner_kernel,
        out_shape=jax.ShapeDtypeStruct((2 * PIECES, NF, LANES), F32),
        in_specs=[pl.BlockSpec(memory_space=pl.ANY)] * 2,
        out_specs=vmem,
        scratch_shapes=[
            pltpu.VMEM((ROWS, COLS, NT), F32),
            pltpu.VMEM((NT, 2 * LANES), BF16),
            pltpu.VMEM((8 * COLS, LANES), F32),
            pltpu.VMEM((2 * PIECES, NF, LANES), F32),
            pltpu.VMEM((2 * PIECES, GROUP, LANES), F32),
            pltpu.VMEM((2, SIZE, SIZE), F32),
            pltpu.VMEM((SIZE, 2 * SIZE), F32),
            pltpu.VMEM((2 * SIZE, 2 * SIZE), BF16),
            pltpu.VMEM((2 * SIZE, 2 * SIZE), BF16),
            pltpu.VMEM((SIZE // 2, 2 * SIZE), F32),
            pltpu.VMEM((2 * PIECES, GROUP, LANES), F32),
            pltpu.SemaphoreType.DMA((4,)),
        ] + [pltpu.SemaphoreType.DMA] * 6,
        compiler_params=pltpu.CompilerParams(
            collective_id=0, has_side_effects=True, vmem_limit_bytes=53 * 2**20
        ),
    )(traces, forward)
    return pl.pallas_call(
        inverse_kernel,
        grid=(3,),
        out_shape=jax.ShapeDtypeStruct((ROWS, COLS, NT), F32),
        in_specs=[vmem, vmem],
        out_specs=pl.BlockSpec((8, COLS, NT), lambda third: (third, 0, 0)),
        scratch_shapes=[pltpu.VMEM((LANES, LANES), F32)],
        compiler_params=pltpu.CompilerParams(vmem_limit_bytes=20 * 2**20),
    )(back, inverse)


def solution(mesh):
    forward, inverse = tables()
    spec = P(("band", "shot"), "recv", None)
    return jax.shard_map(
        functools.partial(body, jnp.asarray(forward), jnp.asarray(inverse)),
        mesh=mesh, in_specs=(spec,), out_specs=spec, check_vma=False,
    )
```

```python
import functools
import math
import random

import jax
import jax.numpy as jnp
import numpy as np
from jax import lax
from jax.experimental import pallas as pl
from jax.experimental.pallas import tpu as pltpu
from jax.sharding import PartitionSpec as P

K0 = 32
NT = 512
NF = 64
SIZE = 384
SHOTS = 16
RECVS = 8
GROUP = SHOTS * RECVS
ROWS = SIZE // SHOTS
COLS = SIZE // RECVS
LANES = 128
PIECES = 9
F32 = jnp.float32
BF16 = jnp.bfloat16
MESH = pl.DeviceIdType.MESH


def ring(offset):
    return min(offset, 8 - offset)


def far_first(kept):
    offsets = [(x, y, z) for x in range(2) for y in range(8) for z in range(8) if kept(x, y, z)]
    random.Random(7).shuffle(offsets)
    return sorted(offsets, key=lambda o: -(2 * o[0] + ring(o[1]) + ring(o[2])))


GREET_ORDER = far_first(lambda x, y, z: True)[:-1]
SEND_ORDER = [far_first(lambda x, y, z: (y + z) % 2 == odd) for odd in range(2)]
REPLY_ORDER = [far_first(lambda x, y, z: y % 2 == odd) for odd in range(2)]


def split_np(table):
    high = table.astype(BF16)
    low = (table - high.astype(np.float32)).astype(BF16)
    return high, low


def tables():
    times = np.arange(NT)
    bins = np.arange(NF) + K0
    angles = (times[:, None] * bins[None, :] % NT) * (2.0 * math.pi / NT)
    cosines, sines = np.cos(angles), np.sin(angles)
    forward = np.concatenate([cosines, -sines], axis=1) / math.sqrt(NT * SIZE)
    inverse = np.concatenate([cosines.T, -sines.T], axis=0) * (2.0 * math.sqrt(SIZE / NT))
    f_high, f_low = split_np(forward.astype(np.float32))
    i_high, i_low = split_np(inverse.astype(np.float32))
    return np.concatenate([f_high, f_low], axis=1), np.concatenate([i_high, i_high, i_low], axis=0)


def split(value):
    high = value.astype(BF16)
    low = (value - high.astype(F32)).astype(BF16)
    return high, low


def dot(a, b):
    return jnp.dot(a, b, preferred_element_type=F32)


def exchange(regs):
    lane = lax.broadcasted_iota(jnp.int32, (8, LANES), 1)
    for bit in (1, 2, 4):
        upper = (lane & bit) != 0
        fresh = list(regs)
        for v in range(8):
            if v & bit:
                continue
            low, high = regs[v], regs[v | bit]
            fresh[v] = jnp.where(upper, pltpu.roll(high, bit, 1), low)
            fresh[v | bit] = jnp.where(upper, high, pltpu.roll(low, LANES - bit, 1))
        regs = fresh
    return regs


def owner_kernel(
    traces, table_hbm, back,
    tile, table, spec, stage, land, raw, sym, w_high, w_low, total, leave,
    load_sem, send_sem, recv_sem, own_sem, send2_sem, recv2_sem, own2_sem,
):
    band, shot, recv = lax.axis_index("band"), lax.axis_index("shot"), lax.axis_index("recv")
    parity = lax.rem(band, 2)
    x_hi, y_at = shot // 8, lax.rem(shot, 8)
    is_owner = lax.rem(shot + recv + parity, 2) == 0
    my_bin = shot * 4 + recv // 2
    my_slot = (lax.rem(shot, 2) * 8 + recv) * 8 + shot // 2

    loads = [pltpu.make_async_copy(table_hbm, table, load_sem.at[3])]
    loads[0].start()
    for third in range(3):
        part = pl.ds(third * 8, 8)
        loads.append(pltpu.make_async_copy(traces.at[part], tile.at[part], load_sem.at[third]))
        loads[-1].start()

    barrier = pltpu.get_barrier_semaphore()

    def device(x, y, z):
        return (lax.rem(x_hi + x, 2) * 8 + lax.rem(y_at + y, 8), lax.rem(recv + z, 8))

    def pick(odd, orders, k):
        even, uneven = orders[0][k], orders[1][k]
        return [a if a == b else jnp.where(odd == 0, a, b) for a, b in zip(even, uneven)]

    for offset in GREET_ORDER:
        to_shot, to_recv = device(*offset)
        pl.semaphore_signal(barrier, inc=1, device_id=(band, to_shot, to_recv), device_id_type=MESH)

    loads[0].wait()
    for third in range(3):
        loads[third + 1].wait()
        x_high, x_low = split(tile[pl.ds(third * 8, 8)].reshape(8 * COLS, NT))
        wide = dot(x_high, table[...])
        spec[...] = wide[:, :LANES] + wide[:, LANES:] + dot(x_low, table[:, :LANES])
        for c in range(3):
            rows = [spec[pl.ds(16 * c + m, 8, stride=COLS), :] for m in range(16)]
            turned = jnp.concatenate(rows, axis=0).T
            stage[third * 3 + c] = turned[:NF]
            stage[PIECES + third * 3 + c] = turned[NF:]

    pl.semaphore_wait(barrier, GROUP - 1)

    @pl.when(is_owner)
    def _():
        pltpu.make_async_copy(stage.at[:, my_bin, :], land.at[:, my_slot, :], own_sem).start()

    def send(x, y, z):
        to_shot, to_recv = device(x, y, z)
        pltpu.make_async_remote_copy(
            src_ref=stage.at[:, to_shot * 4 + to_recv // 2, :], dst_ref=land.at[:, my_slot, :],
            send_sem=send_sem, recv_sem=recv_sem, device_id=(band, to_shot, to_recv), device_id_type=MESH,
        ).start()

    odd = lax.rem(shot + recv + parity, 2)
    for k in range(NF - 1):
        send(*pick(odd, SEND_ORDER, k))

    @pl.when(jnp.logical_not(is_owner))
    def _():
        send(*SEND_ORDER[1][NF - 1])

    @pl.when(is_owner)
    def _():
        one = land.at[:, 0, :]
        pltpu.make_async_copy(one, one, own_sem).wait()
        rest = land.at[:, pl.ds(0, GROUP - 1), :]
        pltpu.make_async_copy(rest, rest, recv_sem).wait()

        def arrange(block, carry):
            half, third = block // 3, lax.rem(block, 3)
            for comp in range(2):
                for c in range(3):
                    piece = comp * PIECES + third * 3 + c
                    regs = [land[piece, pl.ds(pl.multiple_of((half * 8 + v) * 8, 8), 8), :] for v in range(8)]
                    regs = exchange(regs)
                    for v in range(8):
                        row = pl.multiple_of((half * 24 + third * 8 + v) * 8, 8)
                        raw[comp, pl.ds(row, 8), c * LANES:(c + 1) * LANES] = regs[v]
            return carry

        lax.fori_loop(0, 6, arrange, 0)

        for comp in range(2):
            for p in range(3):
                for q in range(3):
                    rows, cols = slice(p * LANES, (p + 1) * LANES), slice(q * LANES, (q + 1) * LANES)
                    value = 0.5 * (raw[comp, rows, cols] + raw[comp, cols, rows].T)
                    high, low = split(value)
                    below = slice(SIZE + p * LANES, SIZE + (p + 1) * LANES)
                    here = slice(comp * SIZE + q * LANES, comp * SIZE + (q + 1) * LANES)
                    there = slice((1 - comp) * SIZE + q * LANES, (1 - comp) * SIZE + (q + 1) * LANES)
                    sym[rows, here] = value
                    w_high[rows, here] = high
                    w_low[rows, here] = low
                    w_high[below, there] = high if comp == 0 else -high
                    w_low[below, there] = low if comp == 0 else -low

        def product(high, low):
            both = dot(jnp.concatenate([high, low], axis=0), w_high[...])
            return both[:SIZE // 2] + both[SIZE // 2:] + dot(high, w_low[...])

        def half_of(turn, carry):
            half = lax.rem(turn + recv, 2)
            mine = pl.ds(pl.multiple_of(half * 192, 64), 192)
            square = product(w_high[mine, :], w_low[mine, :])
            s_high, s_low = split(square)
            total[...] = sym[mine, :] + square + product(s_high, s_low)
            def scatter(third, carry):
                for comp in range(2):
                    for c in range(3):
                        lanes = slice(comp * SIZE + c * LANES, comp * SIZE + (c + 1) * LANES)
                        regs = [total[pl.ds(pl.multiple_of((third * 8 + v) * 8, 8), 8), lanes] for v in range(8)]
                        regs = exchange(regs)
                        for v in range(8):
                            slot = pl.ds(pl.multiple_of((half * 8 + v) * 8, 8), 8)
                            leave[comp * PIECES + third * 3 + c, slot, :] = regs[v]
                return carry

            lax.fori_loop(0, 3, scatter, 0)

            def reply(x, y, z):
                to_shot, to_recv = device(x, y, z)
                slot = (half * 8 + to_recv) * 8 + to_shot // 2
                pltpu.make_async_remote_copy(
                    src_ref=leave.at[:, slot, :], dst_ref=back.at[:, my_bin, :],
                    send_sem=send2_sem, recv_sem=recv2_sem, device_id=(band, to_shot, to_recv), device_id_type=MESH,
                ).start()

            apart = lax.rem(half + shot, 2)
            for k in range(63):
                reply(*pick(apart, REPLY_ORDER, k))

            @pl.when(apart == 0)
            def _():
                pltpu.make_async_copy(leave.at[:, my_slot, :], back.at[:, my_bin, :], own2_sem).start()

            @pl.when(apart == 1)
            def _():
                reply(*REPLY_ORDER[1][63])

            return carry

        lax.fori_loop(0, 2, half_of, 0)

        pltpu.make_async_copy(stage.at[:, pl.ds(0, NF - 1), :], stage.at[:, pl.ds(0, NF - 1), :], send_sem).wait()
        one = back.at[:, 0, :]
        pltpu.make_async_copy(one, one, own2_sem).wait()
        rest = back.at[:, pl.ds(0, NF - 1), :]
        pltpu.make_async_copy(rest, rest, recv2_sem).wait()
        rest = leave.at[:, pl.ds(0, GROUP - 1), :]
        pltpu.make_async_copy(rest, rest, send2_sem).wait()

    @pl.when(jnp.logical_not(is_owner))
    def _():
        pltpu.make_async_copy(stage, stage, send_sem).wait()
        pltpu.make_async_copy(back, back, recv2_sem).wait()


def inverse_kernel(back, table, out, turned):
    third = pl.program_id(0)
    for c in range(3):
        both = jnp.concatenate([back[third * 3 + c], back[PIECES + third * 3 + c]], axis=0)
        turned[...] = both.T
        rows = [turned[pl.ds(a, 16, stride=8), :] for a in range(8)]
        high, low = split(jnp.concatenate(rows, axis=0))
        both = jnp.concatenate([high, low], axis=1)
        value = dot(both, table[:2 * LANES, :]) + dot(high, table[2 * LANES:, :])
        out[:, 16 * c:16 * (c + 1), :] = value.reshape(8, 16, NT)


def body(forward, inverse, traces):
    vmem = pl.BlockSpec(memory_space=pltpu.VMEM)
    back = pl.pallas_call(
        owner_kernel,
        out_shape=jax.ShapeDtypeStruct((2 * PIECES, NF, LANES), F32),
        in_specs=[pl.BlockSpec(memory_space=pl.ANY)] * 2,
        out_specs=vmem,
        scratch_shapes=[
            pltpu.VMEM((ROWS, COLS, NT), F32),
            pltpu.VMEM((NT, 2 * LANES), BF16),
            pltpu.VMEM((8 * COLS, LANES), F32),
            pltpu.VMEM((2 * PIECES, NF, LANES), F32),
            pltpu.VMEM((2 * PIECES, GROUP, LANES), F32),
            pltpu.VMEM((2, SIZE, SIZE), F32),
            pltpu.VMEM((SIZE, 2 * SIZE), F32),
            pltpu.VMEM((2 * SIZE, 2 * SIZE), BF16),
            pltpu.VMEM((2 * SIZE, 2 * SIZE), BF16),
            pltpu.VMEM((SIZE // 2, 2 * SIZE), F32),
            pltpu.VMEM((2 * PIECES, GROUP, LANES), F32),
            pltpu.SemaphoreType.DMA((4,)),
        ] + [pltpu.SemaphoreType.DMA] * 6,
        compiler_params=pltpu.CompilerParams(
            collective_id=0, has_side_effects=True, vmem_limit_bytes=53 * 2**20
        ),
    )(traces, forward)
    return pl.pallas_call(
        inverse_kernel,
        grid=(3,),
        out_shape=jax.ShapeDtypeStruct((ROWS, COLS, NT), F32),
        in_specs=[vmem, vmem],
        out_specs=pl.BlockSpec((8, COLS, NT), lambda third: (third, 0, 0)),
        scratch_shapes=[pltpu.VMEM((LANES, LANES), F32)],
        compiler_params=pltpu.CompilerParams(vmem_limit_bytes=20 * 2**20),
    )(back, inverse)


def solution(mesh):
    forward, inverse = tables()
    spec = P(("band", "shot"), "recv", None)
    return jax.shard_map(
        functools.partial(body, jnp.asarray(forward), jnp.asarray(inverse)),
        mesh=mesh, in_specs=(spec,), out_specs=spec, check_vma=False,
    )
```

```python
import functools
import math
import random

import jax
import jax.numpy as jnp
import numpy as np
from jax import lax
from jax.experimental import pallas as pl
from jax.experimental.pallas import tpu as pltpu
from jax.sharding import PartitionSpec as P

K0 = 32
NT = 512
NF = 64
SIZE = 384
SHOTS = 16
RECVS = 8
GROUP = SHOTS * RECVS
ROWS = SIZE // SHOTS
COLS = SIZE // RECVS
LANES = 128
PIECES = 9
TABLE_ROWS = 8192
F32 = jnp.float32
BF16 = jnp.bfloat16
MESH = pl.DeviceIdType.MESH


def ring(offset):
    return min(offset, 8 - offset)


def far_first(kept):
    offsets = [(x, y, z) for x in range(2) for y in range(8) for z in range(8) if kept(x, y, z)]
    random.Random(7).shuffle(offsets)
    return sorted(offsets, key=lambda o: -(2 * o[0] + ring(o[1]) + ring(o[2])))


GREET_ORDER = far_first(lambda x, y, z: True)[:-1]
SEND_ORDER = [far_first(lambda x, y, z: (y + z) % 2 == odd) for odd in range(2)]
REPLY_ORDER = [far_first(lambda x, y, z: y % 2 == odd) for odd in range(2)]


def split_np(table):
    high = table.astype(BF16)
    low = (table - high.astype(np.float32)).astype(BF16)
    return high, low


def tables():
    times = np.arange(NT)
    bins = np.arange(NF) + K0
    angles = (times[:, None] * bins[None, :] % NT) * (2.0 * math.pi / NT)
    cosines, sines = np.cos(angles), np.sin(angles)
    forward = np.concatenate([cosines, -sines], axis=1) / math.sqrt(NT * SIZE)
    inverse = np.concatenate([cosines.T, -sines.T], axis=0) * (2.0 * math.sqrt(SIZE / NT))
    f_high, f_low = split_np(forward.astype(np.float32))
    i_high, i_low = split_np(inverse.astype(np.float32))
    f_both = np.zeros((TABLE_ROWS, 2 * LANES), BF16)
    f_both[:NT] = np.concatenate([f_high, f_low], axis=1)
    return f_both, np.concatenate([i_high, i_high, i_low], axis=0)


def split(value):
    high = value.astype(BF16)
    low = (value - high.astype(F32)).astype(BF16)
    return high, low


def dot(a, b):
    return jnp.dot(a, b, preferred_element_type=F32)


def exchange(regs):
    lane = lax.broadcasted_iota(jnp.int32, (8, LANES), 1)
    regs = [pltpu.roll(reg, v, 1) if v else reg for v, reg in enumerate(regs)]
    for bit in (1, 2, 4):
        upper = (lane & bit) != 0
        regs = [jnp.where(upper, regs[(v + bit) % 8], regs[v]) for v in range(8)]
    return [pltpu.roll(regs[8 - v], LANES - v, 1) if v else regs[0] for v in range(8)]


def owner_kernel(
    traces, table_hbm, back,
    tile, table, spec, stage, land, raw, sym, w_high, w_low, total, leave,
    load_sem, send_sem, recv_sem, own_sem, send2_sem, recv2_sem, own2_sem,
):
    band, shot, recv = lax.axis_index("band"), lax.axis_index("shot"), lax.axis_index("recv")
    parity = lax.rem(band, 2)
    x_hi, y_at = shot // 8, lax.rem(shot, 8)
    is_owner = lax.rem(shot + recv + parity, 2) == 0
    my_bin = shot * 4 + recv // 2
    my_slot = (lax.rem(shot, 2) * 8 + recv) * 8 + shot // 2

    loads = [pltpu.make_async_copy(table_hbm.at[pl.ds(0, NT)], table, load_sem.at[3])]
    loads[0].start()
    for third in range(3):
        part = pl.ds(third * 8, 8)
        loads.append(pltpu.make_async_copy(traces.at[part], tile.at[part], load_sem.at[third]))
        loads[-1].start()

    barrier = pltpu.get_barrier_semaphore()

    def device(x, y, z):
        return (lax.rem(x_hi + x, 2) * 8 + lax.rem(y_at + y, 8), lax.rem(recv + z, 8))

    def pick(odd, orders, k):
        even, uneven = orders[0][k], orders[1][k]
        return [a if a == b else jnp.where(odd == 0, a, b) for a, b in zip(even, uneven)]

    for offset in GREET_ORDER:
        to_shot, to_recv = device(*offset)
        pl.semaphore_signal(barrier, inc=1, device_id=(band, to_shot, to_recv), device_id_type=MESH)

    loads[0].wait()
    for third in range(3):
        loads[third + 1].wait()
        x_high, x_low = split(tile[pl.ds(third * 8, 8)].reshape(8 * COLS, NT))
        wide = dot(x_high, table[...])
        spec[...] = wide[:, :LANES] + wide[:, LANES:] + dot(x_low, table[:, :LANES])
        for c in range(3):
            rows = [spec[pl.ds(16 * c + m, 8, stride=COLS), :] for m in range(16)]
            turned = jnp.concatenate(rows, axis=0).T
            stage[third * 3 + c] = turned[:NF]
            stage[PIECES + third * 3 + c] = turned[NF:]

    pl.semaphore_wait(barrier, GROUP - 1)

    @pl.when(is_owner)
    def _():
        pltpu.make_async_copy(stage.at[:, my_bin, :], land.at[:, my_slot, :], own_sem).start()

    def send(x, y, z):
        to_shot, to_recv = device(x, y, z)
        pltpu.make_async_remote_copy(
            src_ref=stage.at[:, to_shot * 4 + to_recv // 2, :], dst_ref=land.at[:, my_slot, :],
            send_sem=send_sem, recv_sem=recv_sem, device_id=(band, to_shot, to_recv), device_id_type=MESH,
        ).start()

    odd = lax.rem(shot + recv + parity, 2)
    for k in range(NF - 1):
        send(*pick(odd, SEND_ORDER, k))

    @pl.when(jnp.logical_not(is_owner))
    def _():
        send(*SEND_ORDER[1][NF - 1])

    @pl.when(is_owner)
    def _():
        one = land.at[:, 0, :]
        pltpu.make_async_copy(one, one, own_sem).wait()
        rest = land.at[:, pl.ds(0, GROUP - 1), :]
        pltpu.make_async_copy(rest, rest, recv_sem).wait()

        def arrange(block, carry):
            half, third = block // 3, lax.rem(block, 3)
            for comp in range(2):
                for c in range(3):
                    piece = comp * PIECES + third * 3 + c
                    regs = [land[piece, pl.ds(pl.multiple_of((half * 8 + v) * 8, 8), 8), :] for v in range(8)]
                    regs = exchange(regs)
                    for v in range(8):
                        row = pl.multiple_of((half * 24 + third * 8 + v) * 8, 8)
                        raw[comp, pl.ds(row, 8), c * LANES:(c + 1) * LANES] = regs[v]
            return carry

        lax.fori_loop(0, 6, arrange, 0)

        for comp in range(2):
            for p in range(3):
                for q in range(3):
                    rows, cols = slice(p * LANES, (p + 1) * LANES), slice(q * LANES, (q + 1) * LANES)
                    value = 0.5 * (raw[comp, rows, cols] + raw[comp, cols, rows].T)
                    high, low = split(value)
                    below = slice(SIZE + p * LANES, SIZE + (p + 1) * LANES)
                    here = slice(comp * SIZE + q * LANES, comp * SIZE + (q + 1) * LANES)
                    there = slice((1 - comp) * SIZE + q * LANES, (1 - comp) * SIZE + (q + 1) * LANES)
                    sym[rows, here] = value
                    w_high[rows, here] = high
                    w_low[rows, here] = low
                    w_high[below, there] = high if comp == 0 else -high
                    w_low[below, there] = low if comp == 0 else -low

        def product(high, low):
            both = dot(jnp.concatenate([high, low], axis=0), w_high[...])
            return both[:SIZE // 2] + both[SIZE // 2:] + dot(high, w_low[...])

        def half_of(turn, carry):
            half = lax.rem(turn + recv, 2)
            mine = pl.ds(pl.multiple_of(half * 192, 64), 192)
            square = product(w_high[mine, :], w_low[mine, :])
            s_high, s_low = split(square)
            total[...] = sym[mine, :] + square + product(s_high, s_low)
            def scatter(third, carry):
                for comp in range(2):
                    for c in range(3):
                        lanes = slice(comp * SIZE + c * LANES, comp * SIZE + (c + 1) * LANES)
                        regs = [total[pl.ds(pl.multiple_of((third * 8 + v) * 8, 8), 8), lanes] for v in range(8)]
                        regs = exchange(regs)
                        for v in range(8):
                            slot = pl.ds(pl.multiple_of((half * 8 + v) * 8, 8), 8)
                            leave[comp * PIECES + third * 3 + c, slot, :] = regs[v]
                return carry

            lax.fori_loop(0, 3, scatter, 0)

            def reply(x, y, z):
                to_shot, to_recv = device(x, y, z)
                slot = (half * 8 + to_recv) * 8 + to_shot // 2
                pltpu.make_async_remote_copy(
                    src_ref=leave.at[:, slot, :], dst_ref=back.at[:, my_bin, :],
                    send_sem=send2_sem, recv_sem=recv2_sem, device_id=(band, to_shot, to_recv), device_id_type=MESH,
                ).start()

            apart = lax.rem(half + shot, 2)
            for k in range(63):
                reply(*pick(apart, REPLY_ORDER, k))

            @pl.when(apart == 0)
            def _():
                pltpu.make_async_copy(leave.at[:, my_slot, :], back.at[:, my_bin, :], own2_sem).start()

            @pl.when(apart == 1)
            def _():
                reply(*REPLY_ORDER[1][63])

            return carry

        lax.fori_loop(0, 2, half_of, 0)

        pltpu.make_async_copy(stage.at[:, pl.ds(0, NF - 1), :], stage.at[:, pl.ds(0, NF - 1), :], send_sem).wait()
        one = back.at[:, 0, :]
        pltpu.make_async_copy(one, one, own2_sem).wait()
        rest = back.at[:, pl.ds(0, NF - 1), :]
        pltpu.make_async_copy(rest, rest, recv2_sem).wait()
        rest = leave.at[:, pl.ds(0, GROUP - 1), :]
        pltpu.make_async_copy(rest, rest, send2_sem).wait()

    @pl.when(jnp.logical_not(is_owner))
    def _():
        pltpu.make_async_copy(stage, stage, send_sem).wait()
        pltpu.make_async_copy(back, back, recv2_sem).wait()


def inverse_kernel(back, table, out, turned, built, store_sem):
    stores = []
    for third in range(3):
        for c in range(3):
            piece = third * 3 + c
            turned[piece] = jnp.concatenate([back[piece], back[PIECES + piece]], axis=0).T
            rows = [turned[piece, pl.ds(a, 16, stride=8), :] for a in range(8)]
            high, low = split(jnp.concatenate(rows, axis=0))
            both = jnp.concatenate([high, low], axis=1)
            value = dot(both, table[:2 * LANES, :]) + dot(high, table[2 * LANES:, :])
            built[third * 8:(third + 1) * 8, 16 * c:16 * (c + 1), :] = value.reshape(8, 16, NT)
        part = pl.ds(third * 8, 8)
        stores.append(pltpu.make_async_copy(built.at[part], out.at[part], store_sem.at[third]))
        stores[-1].start()
    for store in stores:
        store.wait()


def body(forward, inverse, traces):
    vmem = pl.BlockSpec(memory_space=pltpu.VMEM)
    back = pl.pallas_call(
        owner_kernel,
        out_shape=jax.ShapeDtypeStruct((2 * PIECES, NF, LANES), F32),
        in_specs=[pl.BlockSpec(memory_space=pl.ANY)] * 2,
        out_specs=vmem,
        scratch_shapes=[
            pltpu.VMEM((ROWS, COLS, NT), F32),
            pltpu.VMEM((NT, 2 * LANES), BF16),
            pltpu.VMEM((8 * COLS, LANES), F32),
            pltpu.VMEM((2 * PIECES, NF, LANES), F32),
            pltpu.VMEM((2 * PIECES, GROUP, LANES), F32),
            pltpu.VMEM((2, SIZE, SIZE), F32),
            pltpu.VMEM((SIZE, 2 * SIZE), F32),
            pltpu.VMEM((2 * SIZE, 2 * SIZE), BF16),
            pltpu.VMEM((2 * SIZE, 2 * SIZE), BF16),
            pltpu.VMEM((SIZE // 2, 2 * SIZE), F32),
            pltpu.VMEM((2 * PIECES, GROUP, LANES), F32),
            pltpu.SemaphoreType.DMA((4,)),
        ] + [pltpu.SemaphoreType.DMA] * 6,
        compiler_params=pltpu.CompilerParams(
            collective_id=0, has_side_effects=True, vmem_limit_bytes=53 * 2**20
        ),
    )(traces, forward)
    return pl.pallas_call(
        inverse_kernel,
        out_shape=jax.ShapeDtypeStruct((ROWS, COLS, NT), F32),
        in_specs=[vmem, vmem],
        out_specs=pl.BlockSpec(memory_space=pl.ANY),
        scratch_shapes=[
            pltpu.VMEM((PIECES, LANES, LANES), F32),
            pltpu.VMEM((ROWS, COLS, NT), F32),
            pltpu.SemaphoreType.DMA((3,)),
        ],
        compiler_params=pltpu.CompilerParams(vmem_limit_bytes=20 * 2**20),
    )(back, inverse)


def solution(mesh):
    forward, inverse = tables()
    spec = P(("band", "shot"), "recv", None)
    return jax.shard_map(
        functools.partial(body, jnp.asarray(forward), jnp.asarray(inverse)),
        mesh=mesh, in_specs=(spec,), out_specs=spec, check_vma=False,
    )
```

```python
import functools
import math
import random

import jax
import jax.numpy as jnp
import numpy as np
from jax import lax
from jax.experimental import pallas as pl
from jax.experimental.pallas import tpu as pltpu
from jax.sharding import PartitionSpec as P

K0 = 32
NT = 512
NF = 64
SIZE = 384
SHOTS = 16
RECVS = 8
GROUP = SHOTS * RECVS
ROWS = SIZE // SHOTS
COLS = SIZE // RECVS
LANES = 128
PIECES = 9
TABLE_ROWS = 8192
F32 = jnp.float32
BF16 = jnp.bfloat16
MESH = pl.DeviceIdType.MESH


def ring(offset):
    return min(offset, 8 - offset)


def far_first(kept):
    offsets = [(x, y, z) for x in range(2) for y in range(8) for z in range(8) if kept(x, y, z)]
    random.Random(7).shuffle(offsets)
    return sorted(offsets, key=lambda o: -(2 * o[0] + ring(o[1]) + ring(o[2])))


GREET_ORDER = far_first(lambda x, y, z: True)[:-1]
SEND_ORDER = [far_first(lambda x, y, z: (y + z) % 2 == odd) for odd in range(2)]
REPLY_ORDER = [far_first(lambda x, y, z: y % 2 == odd) for odd in range(2)]


def split_np(table):
    high = table.astype(BF16)
    low = (table - high.astype(np.float32)).astype(BF16)
    return high, low


def tables():
    times = np.arange(NT)
    bins = np.arange(NF) + K0
    angles = (times[:, None] * bins[None, :] % NT) * (2.0 * math.pi / NT)
    cosines, sines = np.cos(angles), np.sin(angles)
    forward = np.concatenate([cosines, -sines], axis=1) / math.sqrt(NT * SIZE)
    inverse = np.concatenate([cosines.T, -sines.T], axis=0) * (2.0 * math.sqrt(SIZE / NT))
    f_high, f_low = split_np(forward.astype(np.float32))
    i_high, i_low = split_np(inverse.astype(np.float32))
    f_both = np.zeros((TABLE_ROWS, 2 * LANES), BF16)
    f_both[:NT] = np.concatenate([f_high, f_low], axis=1)
    return f_both, np.concatenate([i_high, i_high, i_low], axis=0)


def split(value):
    high = value.astype(BF16)
    low = (value - high.astype(F32)).astype(BF16)
    return high, low


def dot(a, b):
    return jnp.dot(a, b, preferred_element_type=F32)


def exchange(regs):
    lane = lax.broadcasted_iota(jnp.int32, (8, LANES), 1)
    regs = [pltpu.roll(reg, v, 1) if v else reg for v, reg in enumerate(regs)]
    for bit in (1, 2, 4):
        upper = (lane & bit) != 0
        regs = [jnp.where(upper, regs[(v + bit) % 8], regs[v]) for v in range(8)]
    return [pltpu.roll(regs[8 - v], LANES - v, 1) if v else regs[0] for v in range(8)]


def owner_kernel(
    traces, table_hbm, back,
    tile, table, spec, stage, land, raw, sym, w_high, w_low, total, leave,
    load_sem, send_sem, recv_sem, own_sem, send2_sem, recv2_sem, own2_sem,
):
    band, shot, recv = lax.axis_index("band"), lax.axis_index("shot"), lax.axis_index("recv")
    parity = lax.rem(band, 2)
    x_hi, y_at = shot // 8, lax.rem(shot, 8)
    is_owner = lax.rem(shot + recv + parity, 2) == 0
    my_bin = shot * 4 + recv // 2
    my_slot = (lax.rem(shot, 2) * 8 + recv) * 8 + shot // 2

    loads = [pltpu.make_async_copy(table_hbm.at[pl.ds(0, NT)], table, load_sem.at[3])]
    loads[0].start()
    for third in range(3):
        part = pl.ds(third * 8, 8)
        loads.append(pltpu.make_async_copy(traces.at[part], tile.at[part], load_sem.at[third]))
        loads[-1].start()

    barrier = pltpu.get_barrier_semaphore()

    def device(x, y, z):
        return (lax.rem(x_hi + x, 2) * 8 + lax.rem(y_at + y, 8), lax.rem(recv + z, 8))

    def pick(odd, orders, k):
        even, uneven = orders[0][k], orders[1][k]
        return [a if a == b else jnp.where(odd == 0, a, b) for a, b in zip(even, uneven)]

    for offset in GREET_ORDER:
        to_shot, to_recv = device(*offset)
        pl.semaphore_signal(barrier, inc=1, device_id=(band, to_shot, to_recv), device_id_type=MESH)

    loads[0].wait()
    for third in range(3):
        loads[third + 1].wait()
        x_high, x_low = split(tile[pl.ds(third * 8, 8)].reshape(8 * COLS, NT))
        wide = dot(x_high, table[...])
        spec[...] = wide[:, :LANES] + wide[:, LANES:] + dot(x_low, table[:, :LANES])
        for c in range(3):
            rows = [spec[pl.ds(16 * c + m, 8, stride=COLS), :] for m in range(16)]
            turned = jnp.concatenate(rows, axis=0).T
            stage[third * 3 + c] = turned[:NF]
            stage[PIECES + third * 3 + c] = turned[NF:]

    pl.semaphore_wait(barrier, GROUP - 1)

    @pl.when(is_owner)
    def _():
        pltpu.make_async_copy(stage.at[:, my_bin, :], land.at[:, my_slot, :], own_sem).start()

    def send(x, y, z):
        to_shot, to_recv = device(x, y, z)
        pltpu.make_async_remote_copy(
            src_ref=stage.at[:, to_shot * 4 + to_recv // 2, :], dst_ref=land.at[:, my_slot, :],
            send_sem=send_sem, recv_sem=recv_sem.at[lax.rem(shot, 2)], device_id=(band, to_shot, to_recv), device_id_type=MESH,
        ).start()

    odd = lax.rem(shot + recv + parity, 2)
    for k in range(NF - 1):
        send(*pick(odd, SEND_ORDER, k))

    @pl.when(jnp.logical_not(is_owner))
    def _():
        send(*SEND_ORDER[1][NF - 1])

    @pl.when(is_owner)
    def _():
        one = land.at[:, 0, :]
        pltpu.make_async_copy(one, one, own_sem).wait()

        def arrived(half):
            for count in (NF - 1, NF):
                @pl.when((lax.rem(shot, 2) == half) == (count < NF))
                def _():
                    rest = land.at[:, pl.ds(half * NF, count), :]
                    pltpu.make_async_copy(rest, rest, recv_sem.at[half]).wait()

        arrived(1)

        def arrange(block, carry):
            half, third = 1 - block // 3, lax.rem(block, 3)
            for comp in range(2):
                for c in range(3):
                    piece = comp * PIECES + third * 3 + c
                    regs = [land[piece, pl.ds(pl.multiple_of((half * 8 + v) * 8, 8), 8), :] for v in range(8)]
                    regs = exchange(regs)
                    for v in range(8):
                        row = pl.multiple_of((half * 24 + third * 8 + v) * 8, 8)
                        raw[comp, pl.ds(row, 8), c * LANES:(c + 1) * LANES] = regs[v]
            return carry

        lax.fori_loop(0, 3, arrange, 0)
        arrived(0)
        lax.fori_loop(3, 6, arrange, 0)

        for comp in range(2):
            for p in range(3):
                for q in range(3):
                    rows, cols = slice(p * LANES, (p + 1) * LANES), slice(q * LANES, (q + 1) * LANES)
                    value = 0.5 * (raw[comp, rows, cols] + raw[comp, cols, rows].T)
                    high, low = split(value)
                    below = slice(SIZE + p * LANES, SIZE + (p + 1) * LANES)
                    here = slice(comp * SIZE + q * LANES, comp * SIZE + (q + 1) * LANES)
                    there = slice((1 - comp) * SIZE + q * LANES, (1 - comp) * SIZE + (q + 1) * LANES)
                    sym[rows, here] = value
                    w_high[rows, here] = high
                    w_low[rows, here] = low
                    w_high[below, there] = high if comp == 0 else -high
                    w_low[below, there] = low if comp == 0 else -low

        def product(high, low):
            both = dot(jnp.concatenate([high, low], axis=0), w_high[...])
            return both[:SIZE // 2] + both[SIZE // 2:] + dot(high, w_low[...])

        def half_of(turn, carry):
            half = lax.rem(turn + recv, 2)
            mine = pl.ds(pl.multiple_of(half * 192, 64), 192)
            square = product(w_high[mine, :], w_low[mine, :])
            s_high, s_low = split(square)
            total[...] = sym[mine, :] + square + product(s_high, s_low)
            def scatter(third, carry):
                for comp in range(2):
                    for c in range(3):
                        lanes = slice(comp * SIZE + c * LANES, comp * SIZE + (c + 1) * LANES)
                        regs = [total[pl.ds(pl.multiple_of((third * 8 + v) * 8, 8), 8), lanes] for v in range(8)]
                        regs = exchange(regs)
                        for v in range(8):
                            slot = pl.ds(pl.multiple_of((half * 8 + v) * 8, 8), 8)
                            leave[comp * PIECES + third * 3 + c, slot, :] = regs[v]
                return carry

            lax.fori_loop(0, 3, scatter, 0)

            def reply(x, y, z):
                to_shot, to_recv = device(x, y, z)
                slot = (half * 8 + to_recv) * 8 + to_shot // 2
                pltpu.make_async_remote_copy(
                    src_ref=leave.at[:, slot, :], dst_ref=back.at[:, my_bin, :],
                    send_sem=send2_sem, recv_sem=recv2_sem, device_id=(band, to_shot, to_recv), device_id_type=MESH,
                ).start()

            apart = lax.rem(half + shot, 2)
            for k in range(63):
                reply(*pick(apart, REPLY_ORDER, k))

            @pl.when(apart == 0)
            def _():
                pltpu.make_async_copy(leave.at[:, my_slot, :], back.at[:, my_bin, :], own2_sem).start()

            @pl.when(apart == 1)
            def _():
                reply(*REPLY_ORDER[1][63])

            return carry

        lax.fori_loop(0, 2, half_of, 0)

        pltpu.make_async_copy(stage.at[:, pl.ds(0, NF - 1), :], stage.at[:, pl.ds(0, NF - 1), :], send_sem).wait()
        one = back.at[:, 0, :]
        pltpu.make_async_copy(one, one, own2_sem).wait()
        rest = back.at[:, pl.ds(0, NF - 1), :]
        pltpu.make_async_copy(rest, rest, recv2_sem).wait()
        rest = leave.at[:, pl.ds(0, GROUP - 1), :]
        pltpu.make_async_copy(rest, rest, send2_sem).wait()

    @pl.when(jnp.logical_not(is_owner))
    def _():
        pltpu.make_async_copy(stage, stage, send_sem).wait()
        pltpu.make_async_copy(back, back, recv2_sem).wait()


def inverse_kernel(back, table, out, turned, built, store_sem):
    stores = []
    for third in range(3):
        for c in range(3):
            piece = third * 3 + c
            turned[piece] = jnp.concatenate([back[piece], back[PIECES + piece]], axis=0).T
            rows = [turned[piece, pl.ds(a, 16, stride=8), :] for a in range(8)]
            high, low = split(jnp.concatenate(rows, axis=0))
            both = jnp.concatenate([high, low], axis=1)
            value = dot(both, table[:2 * LANES, :]) + dot(high, table[2 * LANES:, :])
            built[third * 8:(third + 1) * 8, 16 * c:16 * (c + 1), :] = value.reshape(8, 16, NT)
        part = pl.ds(third * 8, 8)
        stores.append(pltpu.make_async_copy(built.at[part], out.at[part], store_sem.at[third]))
        stores[-1].start()
    for store in stores:
        store.wait()


def body(forward, inverse, traces):
    vmem = pl.BlockSpec(memory_space=pltpu.VMEM)
    back = pl.pallas_call(
        owner_kernel,
        out_shape=jax.ShapeDtypeStruct((2 * PIECES, NF, LANES), F32),
        in_specs=[pl.BlockSpec(memory_space=pl.ANY)] * 2,
        out_specs=vmem,
        scratch_shapes=[
            pltpu.VMEM((ROWS, COLS, NT), F32),
            pltpu.VMEM((NT, 2 * LANES), BF16),
            pltpu.VMEM((8 * COLS, LANES), F32),
            pltpu.VMEM((2 * PIECES, NF, LANES), F32),
            pltpu.VMEM((2 * PIECES, GROUP, LANES), F32),
            pltpu.VMEM((2, SIZE, SIZE), F32),
            pltpu.VMEM((SIZE, 2 * SIZE), F32),
            pltpu.VMEM((2 * SIZE, 2 * SIZE), BF16),
            pltpu.VMEM((2 * SIZE, 2 * SIZE), BF16),
            pltpu.VMEM((SIZE // 2, 2 * SIZE), F32),
            pltpu.VMEM((2 * PIECES, GROUP, LANES), F32),
            pltpu.SemaphoreType.DMA((4,)),
            pltpu.SemaphoreType.DMA,
            pltpu.SemaphoreType.DMA((2,)),
        ] + [pltpu.SemaphoreType.DMA] * 4,
        compiler_params=pltpu.CompilerParams(
            collective_id=0, has_side_effects=True, vmem_limit_bytes=53 * 2**20
        ),
    )(traces, forward)
    return pl.pallas_call(
        inverse_kernel,
        out_shape=jax.ShapeDtypeStruct((ROWS, COLS, NT), F32),
        in_specs=[vmem, vmem],
        out_specs=pl.BlockSpec(memory_space=pl.ANY),
        scratch_shapes=[
            pltpu.VMEM((PIECES, LANES, LANES), F32),
            pltpu.VMEM((ROWS, COLS, NT), F32),
            pltpu.SemaphoreType.DMA((3,)),
        ],
        compiler_params=pltpu.CompilerParams(vmem_limit_bytes=20 * 2**20),
    )(back, inverse)


def solution(mesh):
    forward, inverse = tables()
    spec = P(("band", "shot"), "recv", None)
    return jax.shard_map(
        functools.partial(body, jnp.asarray(forward), jnp.asarray(inverse)),
        mesh=mesh, in_specs=(spec,), out_specs=spec, check_vma=False,
    )
```

```python
import functools
import math
import random

import jax
import jax.numpy as jnp
import numpy as np
from jax import lax
from jax.experimental import pallas as pl
from jax.experimental.pallas import tpu as pltpu
from jax.sharding import PartitionSpec as P

K0 = 32
NT = 512
NF = 64
SIZE = 384
SHOTS = 16
RECVS = 8
GROUP = SHOTS * RECVS
ROWS = SIZE // SHOTS
COLS = SIZE // RECVS
LANES = 128
PIECES = 9
TABLE_ROWS = 8192
F32 = jnp.float32
BF16 = jnp.bfloat16
MESH = pl.DeviceIdType.MESH


def ring(offset):
    return min(offset, 8 - offset)


def far_first(kept):
    offsets = [(x, y, z) for x in range(2) for y in range(8) for z in range(8) if kept(x, y, z)]
    random.Random(7).shuffle(offsets)
    return sorted(offsets, key=lambda o: -(2 * o[0] + ring(o[1]) + ring(o[2])))


GREET_ORDER = far_first(lambda x, y, z: True)[:-1]
SEND_ORDER = [far_first(lambda x, y, z: (y + z) % 2 == odd) for odd in range(2)]
REPLY_ORDER = [far_first(lambda x, y, z: y % 2 == odd) for odd in range(2)]


def split_np(table):
    high = table.astype(BF16)
    low = (table - high.astype(np.float32)).astype(BF16)
    return high, low


def tables():
    times = np.arange(NT)
    bins = np.arange(NF) + K0
    angles = (times[:, None] * bins[None, :] % NT) * (2.0 * math.pi / NT)
    cosines, sines = np.cos(angles), np.sin(angles)
    forward = np.concatenate([cosines, -sines], axis=1) / math.sqrt(NT * SIZE)
    inverse = np.concatenate([cosines.T, -sines.T], axis=0) * (2.0 * math.sqrt(SIZE / NT))
    f_high, f_low = split_np(forward.astype(np.float32))
    i_high, i_low = split_np(inverse.astype(np.float32))
    f_both = np.zeros((TABLE_ROWS, 2 * LANES), BF16)
    f_both[:NT] = np.concatenate([f_high, f_low], axis=1)
    return f_both, np.concatenate([i_high, i_high, i_low], axis=0)


def split(value):
    high = value.astype(BF16)
    low = (value - high.astype(F32)).astype(BF16)
    return high, low


def dot(a, b):
    return jnp.dot(a, b, preferred_element_type=F32)


def exchange(regs):
    lane = lax.broadcasted_iota(jnp.int32, (8, LANES), 1)
    regs = [pltpu.roll(reg, v, 1) if v else reg for v, reg in enumerate(regs)]
    for bit in (1, 2, 4):
        upper = (lane & bit) != 0
        regs = [jnp.where(upper, regs[(v + bit) % 8], regs[v]) for v in range(8)]
    return [pltpu.roll(regs[8 - v], LANES - v, 1) if v else regs[0] for v in range(8)]


def owner_kernel(
    traces, table_hbm, back,
    tile, table, spec, stage, land, raw, sym, w_high, w_low, total, leave,
    load_sem, send_sem, recv_sem, own_sem, send2_sem, recv2_sem, own2_sem,
):
    band, shot, recv = lax.axis_index("band"), lax.axis_index("shot"), lax.axis_index("recv")
    parity = lax.rem(band, 2)
    x_hi, y_at = shot // 8, lax.rem(shot, 8)
    is_owner = lax.rem(shot + recv + parity, 2) == 0
    my_bin = shot * 4 + recv // 2
    my_slot = (lax.rem(shot, 2) * 8 + recv) * 8 + shot // 2

    loads = [pltpu.make_async_copy(table_hbm.at[pl.ds(0, NT)], table, load_sem.at[3])]
    loads[0].start()
    for third in range(3):
        part = pl.ds(third * 8, 8)
        loads.append(pltpu.make_async_copy(traces.at[part], tile.at[part], load_sem.at[third]))
        loads[-1].start()

    barrier = pltpu.get_barrier_semaphore()

    def device(x, y, z):
        return (lax.rem(x_hi + x, 2) * 8 + lax.rem(y_at + y, 8), lax.rem(recv + z, 8))

    def pick(odd, orders, k):
        even, uneven = orders[0][k], orders[1][k]
        return [a if a == b else jnp.where(odd == 0, a, b) for a, b in zip(even, uneven)]

    for offset in GREET_ORDER:
        to_shot, to_recv = device(*offset)
        pl.semaphore_signal(barrier, inc=1, device_id=(band, to_shot, to_recv), device_id_type=MESH)

    loads[0].wait()
    for third in range(3):
        loads[third + 1].wait()
        x_high, x_low = split(tile[pl.ds(third * 8, 8)].reshape(8 * COLS, NT))
        wide = dot(x_high, table[...])
        spec[...] = wide[:, :LANES] + wide[:, LANES:] + dot(x_low, table[:, :LANES])
        for c in range(3):
            rows = [spec[pl.ds(16 * c + m, 8, stride=COLS), :] for m in range(16)]
            turned = jnp.concatenate(rows, axis=0).T
            stage[third * 3 + c] = turned[:NF]
            stage[PIECES + third * 3 + c] = turned[NF:]

    pl.semaphore_wait(barrier, GROUP - 1)

    @pl.when(is_owner)
    def _():
        pltpu.make_async_copy(stage.at[:, my_bin, :], land.at[:, my_slot, :], own_sem).start()

    def send(x, y, z):
        to_shot, to_recv = device(x, y, z)
        pltpu.make_async_remote_copy(
            src_ref=stage.at[:, to_shot * 4 + to_recv // 2, :], dst_ref=land.at[:, my_slot, :],
            send_sem=send_sem, recv_sem=recv_sem.at[lax.rem(shot, 2)], device_id=(band, to_shot, to_recv), device_id_type=MESH,
        ).start()

    odd = lax.rem(shot + recv + parity, 2)
    for k in range(NF - 1):
        send(*pick(odd, SEND_ORDER, k))

    @pl.when(jnp.logical_not(is_owner))
    def _():
        send(*SEND_ORDER[1][NF - 1])

    @pl.when(is_owner)
    def _():
        one = land.at[:, 0, :]
        pltpu.make_async_copy(one, one, own_sem).wait()

        def arrived(half):
            for count in (NF - 1, NF):
                @pl.when((lax.rem(shot, 2) == half) == (count < NF))
                def _():
                    rest = land.at[:, pl.ds(half * NF, count), :]
                    pltpu.make_async_copy(rest, rest, recv_sem.at[half]).wait()

        arrived(1)

        def arrange(block, carry):
            half, third = 1 - block // 3, lax.rem(block, 3)
            for comp in range(2):
                for c in range(3):
                    piece = comp * PIECES + third * 3 + c
                    regs = [land[piece, pl.ds(pl.multiple_of((half * 8 + v) * 8, 8), 8), :] for v in range(8)]
                    regs = exchange(regs)
                    for v in range(8):
                        row = pl.multiple_of((half * 24 + third * 8 + v) * 8, 8)
                        raw[comp, pl.ds(row, 8), c * LANES:(c + 1) * LANES] = regs[v]
            return carry

        lax.fori_loop(0, 3, arrange, 0)
        arrived(0)
        lax.fori_loop(3, 6, arrange, 0)

        for comp in range(2):
            for p in range(3):
                for q in range(3):
                    rows, cols = slice(p * LANES, (p + 1) * LANES), slice(q * LANES, (q + 1) * LANES)
                    value = 0.5 * (raw[comp, rows, cols] + raw[comp, cols, rows].T)
                    high, low = split(value)
                    below = slice(SIZE + p * LANES, SIZE + (p + 1) * LANES)
                    here = slice(comp * SIZE + q * LANES, comp * SIZE + (q + 1) * LANES)
                    there = slice((1 - comp) * SIZE + q * LANES, (1 - comp) * SIZE + (q + 1) * LANES)
                    sym[rows, here] = value
                    w_high[rows, here] = high
                    w_low[rows, here] = low
                    w_high[below, there] = high if comp == 0 else -high
                    w_low[below, there] = low if comp == 0 else -low

        def product(high, low):
            both = dot(jnp.concatenate([high, low], axis=0), w_high[...])
            return both[:SIZE // 2] + both[SIZE // 2:] + dot(high, w_low[...])

        def half_of(turn, carry):
            half = lax.rem(turn + recv, 2)
            mine = pl.ds(pl.multiple_of(half * 192, 64), 192)
            square = product(w_high[mine, :], w_low[mine, :])
            s_high, s_low = split(square)
            total[...] = sym[mine, :] + square + product(s_high, s_low)
            def scatter(third, carry):
                for comp in range(2):
                    for c in range(3):
                        lanes = slice(comp * SIZE + c * LANES, comp * SIZE + (c + 1) * LANES)
                        regs = [total[pl.ds(pl.multiple_of((third * 8 + v) * 8, 8), 8), lanes] for v in range(8)]
                        regs = exchange(regs)
                        for v in range(8):
                            slot = pl.ds(pl.multiple_of((half * 8 + v) * 8, 8), 8)
                            leave[comp * PIECES + third * 3 + c, slot, :] = regs[v]
                return carry

            lax.fori_loop(0, 3, scatter, 0)

            def reply(x, y, z):
                to_shot, to_recv = device(x, y, z)
                slot = (half * 8 + to_recv) * 8 + to_shot // 2
                pltpu.make_async_remote_copy(
                    src_ref=leave.at[:, slot, :], dst_ref=back.at[:, my_bin, :],
                    send_sem=send2_sem, recv_sem=recv2_sem, device_id=(band, to_shot, to_recv), device_id_type=MESH,
                ).start()

            apart = lax.rem(half + shot, 2)
            for k in range(63):
                reply(*pick(apart, REPLY_ORDER, k))

            @pl.when(apart == 0)
            def _():
                pltpu.make_async_copy(leave.at[:, my_slot, :], back.at[:, my_bin, :], own2_sem).start()

            @pl.when(apart == 1)
            def _():
                reply(*REPLY_ORDER[1][63])

            return carry

        lax.fori_loop(0, 2, half_of, 0)

        pltpu.make_async_copy(stage.at[:, pl.ds(0, NF - 1), :], stage.at[:, pl.ds(0, NF - 1), :], send_sem).wait()
        one = back.at[:, 0, :]
        pltpu.make_async_copy(one, one, own2_sem).wait()
        rest = back.at[:, pl.ds(0, NF - 1), :]
        pltpu.make_async_copy(rest, rest, recv2_sem).wait()
        rest = leave.at[:, pl.ds(0, GROUP - 1), :]
        pltpu.make_async_copy(rest, rest, send2_sem).wait()

    @pl.when(jnp.logical_not(is_owner))
    def _():
        pltpu.make_async_copy(stage, stage, send_sem).wait()
        pltpu.make_async_copy(back, back, recv2_sem).wait()


def inverse_kernel(back, table, out, turned, built, store_sem):
    stores = []
    for third in range(3):
        for c in range(3):
            piece = third * 3 + c
            turned[piece] = jnp.concatenate([back[piece], back[PIECES + piece]], axis=0).T
            rows = [turned[piece, pl.ds(a, 16, stride=8), :] for a in range(8)]
            high, low = split(jnp.concatenate(rows, axis=0))
            both = jnp.concatenate([high, low], axis=1)
            value = dot(both, table[:2 * LANES, :]) + dot(high, table[2 * LANES:, :])
            built[third * 8:(third + 1) * 8, 16 * c:16 * (c + 1), :] = value.reshape(8, 16, NT)
            part = (pl.ds(third * 8, 8), pl.ds(16 * c, 16))
            stores.append(pltpu.make_async_copy(built.at[part], out.at[part], store_sem.at[piece]))
            stores[-1].start()
    for store in stores:
        store.wait()


def body(forward, inverse, traces):
    vmem = pl.BlockSpec(memory_space=pltpu.VMEM)
    back = pl.pallas_call(
        owner_kernel,
        out_shape=jax.ShapeDtypeStruct((2 * PIECES, NF, LANES), F32),
        in_specs=[pl.BlockSpec(memory_space=pl.ANY)] * 2,
        out_specs=vmem,
        scratch_shapes=[
            pltpu.VMEM((ROWS, COLS, NT), F32),
            pltpu.VMEM((NT, 2 * LANES), BF16),
            pltpu.VMEM((8 * COLS, LANES), F32),
            pltpu.VMEM((2 * PIECES, NF, LANES), F32),
            pltpu.VMEM((2 * PIECES, GROUP, LANES), F32),
            pltpu.VMEM((2, SIZE, SIZE), F32),
            pltpu.VMEM((SIZE, 2 * SIZE), F32),
            pltpu.VMEM((2 * SIZE, 2 * SIZE), BF16),
            pltpu.VMEM((2 * SIZE, 2 * SIZE), BF16),
            pltpu.VMEM((SIZE // 2, 2 * SIZE), F32),
            pltpu.VMEM((2 * PIECES, GROUP, LANES), F32),
            pltpu.SemaphoreType.DMA((4,)),
            pltpu.SemaphoreType.DMA,
            pltpu.SemaphoreType.DMA((2,)),
        ] + [pltpu.SemaphoreType.DMA] * 4,
        compiler_params=pltpu.CompilerParams(
            collective_id=0, has_side_effects=True, vmem_limit_bytes=53 * 2**20
        ),
    )(traces, forward)
    return pl.pallas_call(
        inverse_kernel,
        out_shape=jax.ShapeDtypeStruct((ROWS, COLS, NT), F32),
        in_specs=[vmem, vmem],
        out_specs=pl.BlockSpec(memory_space=pl.ANY),
        scratch_shapes=[
            pltpu.VMEM((PIECES, LANES, LANES), F32),
            pltpu.VMEM((ROWS, COLS, NT), F32),
            pltpu.SemaphoreType.DMA((PIECES,)),
        ],
        compiler_params=pltpu.CompilerParams(vmem_limit_bytes=20 * 2**20),
    )(back, inverse)


def solution(mesh):
    forward, inverse = tables()
    spec = P(("band", "shot"), "recv", None)
    return jax.shard_map(
        functools.partial(body, jnp.asarray(forward), jnp.asarray(inverse)),
        mesh=mesh, in_specs=(spec,), out_specs=spec, check_vma=False,
    )
```
